256 devices in a mesh: dp: 64 (over z, y, core), fsdp: 4 (over x).
Axes of the slice: x: 4, y: 4, z: 8, core: 2. Of those that a mesh axis runs over, the one named last changes fastest.
Arguments:
- hidden: bfloat16 [65536, 14336], P(('dp', 'fsdp')), may hold values from -6 to 6
- out_grads: bfloat16 [65536, 8192], P(('dp', 'fsdp')), may hold values from -150 to 150
- in_proj: bfloat16 [64, 14336], P(None, 'fsdp'), may hold values from -0.046875 to 0.046875
- out_proj: bfloat16 [64, 8192], P(None, 'fsdp'), may hold values from -0.0625 to 0.0625
- queries: bfloat16 [256, 4096], P(('dp', 'fsdp')), may hold values from -6 to 6
Outputs:
- scores: float32 [256, 512], P(None, ('dp', 'fsdp'))
The draws below stay inside these ranges and needn't reach their ends.
All inputs are finite; a program needn't handle non-finite values.
Results may differ from the reference program's by a relative error of at most 0.013.
Values may be sent and summed in bfloat16 or wider, within the bound.
A program may use at most 128 MiB of HBM per device.

```python
import jax
import jax.numpy as jnp
from jax import lax

D = 8192
FF = 14336
RANK = 64
NQ = 256
LEN = 128
SKETCH = 4096
TOKENS = 65536


def draw_out_grads(key, part):
    key = jax.random.fold_in(key, 11)
    key_base, key_row, key_col = jax.random.split(key, 3)
    base = jnp.clip(jax.random.normal(key_base, (TOKENS, D), jnp.float32), -5.0, 5.0)
    row_scale = 10.0 ** jax.random.uniform(key_row, (TOKENS, 1), jnp.float32)
    col_scale = 10.0 ** jax.random.uniform(key_col, (1, D), jnp.float32)
    ramp = 1.0 + 2.0 * jnp.arange(TOKENS, dtype=jnp.float32)[:, None] / TOKENS
    return (0.1 * base * row_scale * col_scale * ramp).astype(jnp.bfloat16)


def levels(rng, dims, shards, low, largest):
    level = 1.0
    for dim, blocks in shards:
        heights = jax.random.uniform(jax.random.fold_in(jax.random.fold_in(rng, 6), dim), (blocks,), jnp.float32, low / len(shards), largest / len(shards))
        level = level * jnp.repeat(jnp.exp(heights), dims[dim] // blocks).reshape((-1,) + (1,) * (len(dims) - 1 - dim))
    return level


def scatter_about(own_key, dims, deviation, limit, pieces=(), kind=jnp.bfloat16):
    drawn = jax.random.normal(own_key, dims, jnp.float32) * deviation
    if len(pieces) > 0:
        drawn = levels(own_key, dims, pieces, -0.22, 0.18) * drawn
    return jnp.clip(drawn, min=-limit, max=limit).astype(kind)


def setup_inputs(seed: int = 0) -> dict:
    seeds = jax.random.split(jax.random.key(seed), 6)
    hidden = scatter_about(seeds[0], (TOKENS, FF), 1.0, 6.0, ((0, 256),))
    out_grads = draw_out_grads(jax.random.fold_in(seeds[5], 71), 0)
    in_proj = scatter_about(seeds[2], (RANK, FF), FF ** -0.5, 0.046875, ((1, 4),))
    out_proj = scatter_about(seeds[3], (RANK, D), D ** -0.5, 0.0625, ((1, 4),))
    queries = scatter_about(seeds[4], (NQ, SKETCH), 1.0, 6.0, ((0, 256),))
    return {"hidden": hidden, "out_grads": out_grads, "in_proj": in_proj, "out_proj": out_proj, "queries": queries}


def project(rows, matrix):
    return lax.dot_general(rows.astype(jnp.float32), matrix.astype(jnp.float32), (((1,), (1,)), ((), ())), preferred_element_type=jnp.float32)

def reference(hidden, out_grads, in_proj, out_proj, queries):
    in_side = project(hidden, in_proj)
    out_side = project(out_grads, out_proj)
    examples = in_side.shape[0] // LEN
    in_blocks = in_side.reshape(examples, LEN, RANK)
    out_blocks = out_side.reshape(examples, LEN, RANK)
    outer = jnp.einsum('slb,sla->sba', out_blocks, in_blocks) / jnp.sqrt(jnp.float32(LEN))
    sketch = outer.reshape(examples, RANK * RANK).astype(jnp.bfloat16)
    wide = sketch.astype(jnp.float32)
    trace_value = jnp.sum(wide * wide)
    damping = 0.1 * trace_value / examples
    gram = project(sketch, sketch)
    cross = project(sketch, queries)
    system = gram + damping * jnp.eye(examples, dtype=jnp.float32)
    factor = jnp.linalg.cholesky(system)
    middle = lax.linalg.triangular_solve(factor, cross, left_side=True, lower=True)
    solved = lax.linalg.triangular_solve(factor, middle, left_side=True, lower=True, transpose_a=True)
    return damping / RANK * solved.T
```

```python
import functools
import jax
import jax.numpy as jnp
from jax import lax
from jax.experimental import pallas as pl
from jax.experimental.pallas import tpu as pltpu
from jax.sharding import PartitionSpec as P

LEN = 128

f32, bf16 = jnp.float32, jnp.bfloat16


def dot(a, b, precision=None):
    return lax.dot_general(
        a, b, (((1,), (0,)), ((), ())), preferred_element_type=f32, precision=precision
    )


def split(value):
    high = value.astype(bf16)
    return high, (value - high.astype(f32)).astype(bf16)


def solve_kernel(rows_of, rank, gram_ref, cross_ref, out_ref, product, inverse, sys_high, sys_low, answer):
    n = gram_ref.shape[0]
    gram = gram_ref[...]
    row = lax.broadcasted_iota(jnp.int32, (n, n), 0)
    col = lax.broadcasted_iota(jnp.int32, (n, n), 1)
    diagonal = row == col
    trace = jnp.sum(jnp.where(diagonal, gram, 0.0))
    damping = 0.1 * trace / n
    top = damping + jnp.minimum(trace, jnp.max(jnp.sum(jnp.abs(gram), axis=0)))
    system = gram + jnp.where(diagonal, damping, 0.0)
    scale = 2.0 / (damping + top)
    bound0 = (top - damping) / (top + damping)
    high, low = split(system)
    sys_high[...] = high
    sys_low[...] = low
    first, second = rows_of()
    shape = (8, n)
    want_row = lax.broadcasted_iota(jnp.int32, shape, 0)
    want_col = lax.broadcasted_iota(jnp.int32, shape, 1)
    unit = jnp.where(
        ((want_row == 0) & (want_col == first)) | ((want_row == 1) & (want_col == second)), 1.0, 0.0
    )

    def invert(multiply):
        def gain_of(bound):
            return 2.0 / (2.0 - bound * bound)

        def step(bound):
            gain = gain_of(bound)
            y = product[...]
            x = inverse[...]
            inverse[...] = gain * (2.0 * x - multiply(x, y))
            product[...] = gain * (2.0 * y - multiply(y, y))
            return bound * bound * 0.5 * gain

        gain = gain_of(bound0)
        y = scale * system
        inverse[...] = (gain * scale) * (jnp.where(diagonal, 2.0, 0.0) - y)
        product[...] = gain * (2.0 * y - multiply(y, y))
        lax.while_loop(lambda b: b > 0.06, step, bound0 * bound0 * 0.5 * gain)

    def apply(z, high, low):
        parts = jnp.concatenate(split(z), axis=0)
        whole = dot(parts, high) + dot(parts, low)
        return whole[:8] + whole[8:]

    def refine(correct, residual):
        def step(carry):
            z, left, _, count = carry
            z = z + correct(left)
            left = unit - residual(z)
            return z, left, jnp.max(jnp.abs(left)), count + 1

        def go_on(carry):
            return (carry[2] > 2e-5) & (carry[3] < 8)

        z, _, error, _ = lax.while_loop(
            go_on, step, (jnp.zeros(shape, f32), unit, jnp.float32(1.0), jnp.int32(0))
        )
        answer[...] = z
        return error

    def quick():
        invert(lambda a, b: dot(a.astype(bf16), b.astype(bf16)))
        near = inverse[...].astype(bf16)

        def correct(left):
            parts = jnp.concatenate(split(left), axis=0)
            moved = dot(parts, near)
            return moved[:8] + moved[8:]

        return refine(correct, lambda z: apply(z, sys_high[...], sys_low[...]))

    def careful():
        exact = lax.Precision.HIGHEST
        invert(lambda a, b: dot(a, b, exact))
        refine(
            lambda left: dot(left, inverse[...], exact),
            lambda z: dot(z, gram_ref[...], exact) + damping * z,
        )

    error = lax.cond(top < 500.0 * damping, quick, lambda: jnp.float32(1.0))
    pl.when(jnp.logical_not(error <= 2e-5))(careful)
    cross_high, cross_low = split(cross_ref[...])
    out_ref[...] = (damping / rank) * apply(answer[...], cross_high, cross_low)


def solve(gram, cross, rows_of, rank):
    n, nq = cross.shape
    return pl.pallas_call(
        functools.partial(solve_kernel, rows_of, rank),
        out_shape=jax.ShapeDtypeStruct((8, nq), f32),
        in_specs=[pl.BlockSpec(memory_space=pltpu.VMEM)] * 2,
        out_specs=pl.BlockSpec(memory_space=pltpu.VMEM),
        scratch_shapes=[
            pltpu.VMEM((n, n), f32),
            pltpu.VMEM((n, n), f32),
            pltpu.VMEM((n, n), bf16),
            pltpu.VMEM((n, n), bf16),
            pltpu.VMEM((8, n), f32),
        ],
        compiler_params=pltpu.CompilerParams(vmem_limit_bytes=40 * 2**20),
        cost_estimate=pl.CostEstimate(flops=2 * 10 * n**3, bytes_accessed=4 * n * (n + nq), transcendentals=0),
    )(gram, cross)


def project(rows, matrix):
    return lax.dot_general(
        rows, matrix, (((1,), (1,)), ((), ())), preferred_element_type=jnp.float32
    )


def shards(hidden, out_grads, in_proj, out_proj, queries):
    row_count = hidden.shape[0]
    sketch_rank = in_proj.shape[0]
    seq_count = row_count // LEN
    columns = hidden
    in_side = project(columns, lax.all_gather(in_proj, "fsdp", axis=1, tiled=True))
    columns = out_grads
    out_side = project(columns, lax.all_gather(out_proj, "fsdp", axis=1, tiled=True))
    in_blocks = in_side.reshape(seq_count, LEN, sketch_rank)
    out_blocks = out_side.reshape(seq_count, LEN, sketch_rank)
    outer = jnp.einsum("slb,sla->sba", out_blocks, in_blocks) / jnp.sqrt(jnp.float32(LEN))
    own_sketch = outer.reshape(seq_count, sketch_rank * sketch_rank).astype(jnp.bfloat16)
    all_queries = lax.all_gather(queries, ("dp", "fsdp"), axis=0, tiled=True)
    all_sketch = lax.all_gather(own_sketch, ("dp", "fsdp"), axis=0, tiled=True)
    gram = project(all_sketch, all_sketch)
    cross = project(all_sketch, all_queries)

    def rows_of():
        first = lax.axis_index(("dp", "fsdp")) * seq_count
        return first, first + 1

    return solve(gram, cross, rows_of, sketch_rank)[:seq_count].T


def solution(mesh):
    in_specs = (
        P(("dp", "fsdp"), None),
        P(("dp", "fsdp"), None),
        P(None, "fsdp"),
        P(None, "fsdp"),
        P(("dp", "fsdp"), None),
    )
    out_specs = P(None, ("dp", "fsdp"))
    return jax.shard_map(shards, mesh=mesh, in_specs=in_specs, out_specs=out_specs, check_vma=False)
```

```python
import functools
import math
import jax
import jax.numpy as jnp
from jax import lax
from jax.experimental import pallas as pl
from jax.experimental.pallas import tpu as pltpu
from jax.sharding import PartitionSpec as P

LEN = 128
RINGS = (4, 4, 8)
MESH = pl.DeviceIdType.MESH
f32, bf16 = jnp.float32, jnp.bfloat16


def dot_rows(a, b, precision=None):
    return lax.dot_general(
        a, b, (((1,), (1,)), ((), ())), preferred_element_type=f32, precision=precision
    )


def place():
    dp = lax.axis_index("dp")
    return lax.axis_index("fsdp"), lax.rem(lax.div(dp, 2), 4), lax.div(dp, 8), lax.rem(dp, 2)


def gather_kernel(
    hidden, grads, w_in, w_out, query,
    gram_out, cross_out,
    hid, grd, win, wout, sketch_all, query_all, gram_own, gram_other, cross_own, cross_other,
    side, first_sent, first_got, spread, q_flat, q_sent, q_pair, q_x, q_y,
    send, got, first_sem, local,
):
    nx, ny, nz = RINGS
    x, y, z, c = place()
    other = 1 - c

    def at(dx=0, dy=0, dz=0, dc=0):
        px, py = lax.rem(x + (dx + nx), nx), lax.rem(y + (dy + ny), ny)
        pz, pc = lax.rem(z + (dz + nz), nz), lax.rem(c + dc, 2)
        return ((pz * ny + py) * 2 + pc, px)

    x_at = [x, lax.rem(x + 3, 4), lax.rem(x + 1, 4), lax.rem(x + 2, 4)]
    y_at = [y, lax.rem(y + 3, 4), lax.rem(y + 1, 4), lax.rem(y + 2, 4)]
    z_at = {k: lax.rem(z + k + nz, nz) for k in range(-4, 5)}

    partners = (
        [(k, 0, 0, 0) for k in (1, 2, 3)]
        + [(0, k, 0, 0) for k in (1, 2, 3)]
        + [(0, 0, k, j) for k in range(nz) for j in range(2) if k + j > 0]
    )
    barrier = pltpu.get_barrier_semaphore()
    for partner in partners:
        pl.semaphore_signal(barrier, inc=1, device_id=at(*partner), device_id_type=MESH)

    in_width, out_width = w_in.shape[1], w_out.shape[1]
    loads = []

    def load(src, dst):
        copy = pltpu.make_async_copy(src, dst, local.at[len(loads)])
        copy.start()
        loads.append(copy)
        return copy

    own_in = load(w_in, win.at[0])
    own_out = load(w_out, wout.at[0])
    hid_loads, grd_loads = [], []
    for k in range(4):
        hid_loads.append(load(hidden.at[:, pl.ds(pl.multiple_of(x_at[k] * in_width, 128), in_width)], hid.at[k]))
        grd_loads.append(load(grads.at[:, pl.ds(pl.multiple_of(x_at[k] * out_width, 128), out_width)], grd.at[k]))

    sent = []
    count = [0]

    def message(src, dst, device, landing):
        number = count[0]
        count[0] += 1
        copy = pltpu.make_async_remote_copy(
            src_ref=src, dst_ref=dst, send_sem=send.at[number], recv_sem=got.at[number],
            device_id=device, device_id_type=MESH,
        )
        copy.start()
        sent.append(copy)
        return pltpu.make_async_remote_copy(
            src_ref=landing, dst_ref=landing, send_sem=send.at[number], recv_sem=got.at[number],
            device_id=device, device_id_type=MESH,
        )

    for b in range(32):
        q_flat[pl.ds(b, 1), :] = query[:, 128 * b : 128 * (b + 1)].astype(f32)
    for h in range(2):
        q_sent[h] = q_flat[pl.ds(16 * h, 16), :].astype(bf16)

    pl.semaphore_wait(barrier, len(partners))

    color = lax.rem(y, 2)
    mine, theirs = pl.ds(pl.multiple_of(32 * c, 32), 32), pl.ds(pl.multiple_of(32 * other, 32), 32)

    class Matrix:
        def __init__(self, source, slots, width):
            self.source, self.slots, self.half, self.quarter = source, slots, width // 2, width // 4

        def columns(self, which, part=None):
            begin = which * self.half
            if part is None:
                return pl.ds(pl.multiple_of(begin, 128), self.half)
            return pl.ds(pl.multiple_of(begin + part * self.quarter, 128), self.quarter)

        def slot(self, k, rows, columns):
            return self.slots.at[k, rows, columns]

    matrices = [Matrix(w_in, win, in_width), Matrix(w_out, wout, out_width)]
    hop = []
    for m in matrices:
        columns = m.columns(color)
        source = m.source.at[mine, columns]
        hop.append((
            message(source, m.slot(1, mine, columns), at(dx=1), m.slot(1, mine, columns)),
            message(source, m.slot(2, mine, columns), at(dx=-1), m.slot(2, mine, columns)),
        ))
    q_a = message(q_sent.at[other], q_pair.at[c], at(dc=1), q_pair.at[other])
    q_pair[c] = q_sent[c]

    q_a.wait_recv()
    q_x[:, x] = q_pair[...]
    q_b = [
        message(q_pair, q_x.at[:, x], at(dx=k), q_x.at[:, lax.rem(x + nx - k, nx)]) for k in (1, 2, 3)
    ]

    own_in.wait()
    hid_loads[0].wait()
    in_side = dot_rows(hid[0], win[0])
    own_out.wait()
    grd_loads[0].wait()
    out_side = dot_rows(wout[0], grd[0])

    for copy in q_b:
        copy.wait_recv()
    q_y[y] = q_x[...]
    q_c = [
        message(q_x, q_y.at[y], at(dy=k), q_y.at[lax.rem(y + ny - k, ny)]) for k in (1, 2, 3)
    ]

    near = []
    sib = {1: [], 2: [], 3: []}
    last = []

    def to_sibling(m, k, columns):
        sib[k].append(
            message(m.slot(k, mine, columns), m.slot(k, mine, columns), at(dc=1), m.slot(k, theirs, columns))
        )

    def to_y(m, k, part):
        step = 1 if part == 0 else -1
        ours, foreign = m.columns(color, part), m.columns(1 - color, part)
        near.append((
            m, k, foreign,
            message(m.slot(k, mine, ours), m.slot(k, mine, ours), at(dy=step), m.slot(k, mine, foreign)),
        ))

    for m, (from_left, from_right) in zip(matrices, hop):
        part0, part1 = m.columns(color, 0), m.columns(color, 1)
        from_left.wait_recv()
        last.append((m, 0, message(m.slot(1, mine, part0), m.slot(3, mine, part0), at(dx=1), m.slot(3, mine, part0))))
        to_y(m, 1, 0)
        to_y(m, 1, 1)
        to_sibling(m, 1, m.columns(color))
        from_right.wait_recv()
        last.append((m, 1, message(m.slot(2, mine, part1), m.slot(3, mine, part1), at(dx=-1), m.slot(3, mine, part1))))
        to_y(m, 2, 0)
        to_y(m, 2, 1)
        to_sibling(m, 2, m.columns(color))

    for copy in q_c:
        copy.wait_recv()
    spread[...] = q_y[...].reshape(ny * 2 * nx * 16, 128).astype(f32)
    q_rows = ny * 2 * nx

    def q_block(k):
        return query_all.at[pl.ds(pl.multiple_of(z_at[k] * q_rows, q_rows), q_rows), :]

    def q_half(k, h):
        return query_all.at[pl.ds(pl.multiple_of(z_at[k] * q_rows + h * (q_rows // 2), q_rows // 2), q_rows // 2), :]

    for b in range(16):
        query_all[pl.ds(pl.multiple_of(z * q_rows, q_rows), q_rows), 128 * b : 128 * (b + 1)] = spread[
            pl.ds(b, q_rows, stride=16), :
        ].astype(bf16)

    def q_step(t):
        if t < 4:
            return (
                message(q_block(1 - t), q_block(1 - t), at(dz=1), q_block(-t)),
                message(q_block(t - 1), q_block(t - 1), at(dz=-1), q_block(t)),
            )
        return (
            message(q_half(-3, 0), q_half(-3, 0), at(dz=1), q_half(-4, 0)),
            message(q_half(3, 1), q_half(3, 1), at(dz=-1), q_half(4, 1)),
        )

    def arrive(pair):
        for copy in pair:
            copy.wait_recv()

    q_ring = q_step(1)

    for m, part, copy in last:
        copy.wait_recv()
        to_y(m, 3, part)
        to_sibling(m, 3, m.columns(color, part))
    arrive(q_ring)
    q_ring = q_step(2)
    for k in (1, 2, 3):
        for m, at_k, columns, copy in near:
            if at_k == k:
                copy.wait_recv()
                to_sibling(m, k, columns)
    for k in (1, 2, 3):
        hid_loads[k].wait()
        grd_loads[k].wait()
        for copy in sib[k]:
            copy.wait_recv()
        in_side += dot_rows(hid[k], win[k])
        out_side += dot_rows(wout[k], grd[k])
        if k == 1:
            arrive(q_ring)
            q_ring = q_step(3)
    arrive(q_ring)
    q_ring = q_step(4)

    exact = lax.Precision.HIGHEST
    rank = in_side.shape[1]
    for s in range(2):
        outer = lax.dot_general(
            out_side[:, LEN * s : LEN * (s + 1)], in_side[LEN * s : LEN * (s + 1), :],
            (((1,), (0,)), ((), ())), preferred_element_type=f32, precision=exact,
        )
        side[...] = outer / math.sqrt(LEN)
        rows = jnp.concatenate(
            [side[pl.ds(0, rank // 2, stride=2), :], side[pl.ds(1, rank // 2, stride=2), :]], axis=1
        ).astype(bf16)
        for h in range(2):
            first_sent[h, 16 * s : 16 * (s + 1), :] = rows[16 * h : 16 * (h + 1), :]

    slot = z * 2 + c
    first = []
    for dz in range(nz):
        for dc in range(2):
            if dz + dc > 0:
                copy = pltpu.make_async_remote_copy(
                    src_ref=first_sent.at[lax.rem(c + dc, 2)], dst_ref=first_got.at[slot],
                    send_sem=send.at[count[0]], recv_sem=first_sem, device_id=at(dz=dz, dc=dc), device_id_type=MESH,
                )
                count[0] += 1
                copy.start()
                sent.append(copy)
    first_got[slot] = first_sent[c]
    everyone = first_got.at[pl.ds(0, 2 * nz - 1)]
    pltpu.make_async_remote_copy(
        src_ref=everyone, dst_ref=everyone, send_sem=send.at[0], recv_sem=first_sem,
        device_id=at(dc=1), device_id_type=MESH,
    ).wait_recv()
    spread[...] = first_got[...].reshape(2 * nz * 32, 128).astype(f32)
    rows = 2 * 2 * nz

    def block(kx, ky):
        return sketch_all.at[pl.ds(pl.multiple_of((kx * ny + ky) * rows, rows), rows), :]

    def half(kx, ky, h):
        return sketch_all.at[pl.ds(pl.multiple_of((kx * ny + ky) * rows + h * (rows // 2), rows // 2), rows // 2), :]

    for s in range(2):
        for b in range(16):
            begin = pl.multiple_of((x * ny + y) * rows + s * 16, 16)
            sketch_all[pl.ds(begin, 16), 128 * b : 128 * (b + 1)] = spread[
                pl.ds(s * 16 + b, 16, stride=32), :
            ].astype(bf16)

    def pick(on_first, on_second):
        return on_first + c * (on_second - on_first)

    u_at = [pick(a, b) for a, b in zip(y_at, x_at)]
    v_at = [pick(a, b) for a, b in zip(x_at, y_at)]

    def cell(u, v):
        return pick(v_at[v], u_at[u]), pick(u_at[u], v_at[v])

    def along_u(step):
        return at(dx=c * step, dy=other * step)

    def along_v(step):
        return at(dx=other * step, dy=c * step)

    u_left = message(block(*cell(0, 0)), block(*cell(0, 0)), along_u(1), block(*cell(1, 0)))
    u_right = message(block(*cell(0, 0)), block(*cell(0, 0)), along_u(-1), block(*cell(2, 0)))

    def send_v(u):
        here = block(*cell(u, 0))
        return (
            message(here, here, along_v(1), block(*cell(u, 1))),
            message(here, here, along_v(-1), block(*cell(u, 2))),
        )

    def forward_v(u, pair):
        pair[0].wait_recv()
        a = half(*cell(u, 1), 0)
        left = message(a, a, along_v(1), half(*cell(u, 3), 0))
        pair[1].wait_recv()
        b = half(*cell(u, 2), 1)
        right = message(b, b, along_v(-1), half(*cell(u, 3), 1))
        return left, right

    v_pairs = {0: send_v(0)}
    u_left.wait_recv()
    a = half(*cell(1, 0), 0)
    u_far = [message(a, a, along_u(1), half(*cell(3, 0), 0))]
    v_pairs[1] = send_v(1)
    u_right.wait_recv()
    b = half(*cell(2, 0), 1)
    u_far.append(message(b, b, along_u(-1), half(*cell(3, 0), 1)))
    v_pairs[2] = send_v(2)
    tails = [forward_v(0, v_pairs[0])]
    arrive(u_far)
    v_pairs[3] = send_v(3)
    arrive(q_ring)
    for u in (1, 2, 3):
        tails.append(forward_v(u, v_pairs[u]))
    for pair in tails:
        arrive(pair)

    gram_own[...] = dot_rows(sketch_all[...], sketch_all[...])
    gram_sum = message(gram_own, gram_other, at(dc=1), gram_other)
    cross_own[...] = dot_rows(sketch_all[...], query_all[...])
    cross_sum = message(cross_own, cross_other, at(dc=1), cross_other)
    gram_sum.wait_recv()
    gram_out[...] = gram_own[...] + gram_other[...]
    cross_sum.wait_recv()
    cross_out[...] = cross_own[...] + cross_other[...]

    for copy in sent:
        copy.wait_send()


def gather(hidden, grads, w_in, w_out, query):
    examples, queries, half = 512, 256, 2048
    rank = w_in.shape[0]
    anywhere = pl.BlockSpec(memory_space=pl.ANY)
    vmem = pl.BlockSpec(memory_space=pltpu.VMEM)
    rows = hidden.shape[0]
    return pl.pallas_call(
        gather_kernel,
        out_shape=(
            jax.ShapeDtypeStruct((examples, examples), f32),
            jax.ShapeDtypeStruct((examples, queries), f32),
        ),
        in_specs=[anywhere] * 4 + [vmem],
        out_specs=(vmem, vmem),
        scratch_shapes=[
            pltpu.VMEM((4, rows, w_in.shape[1]), bf16),
            pltpu.VMEM((4, rows, w_out.shape[1]), bf16),
            pltpu.VMEM((4, rank, w_in.shape[1]), bf16),
            pltpu.VMEM((4, rank, w_out.shape[1]), bf16),
            pltpu.VMEM((examples, half), bf16),
            pltpu.VMEM((queries, half), bf16),
            pltpu.VMEM((examples, examples), f32),
            pltpu.VMEM((examples, examples), f32),
            pltpu.VMEM((examples, queries), f32),
            pltpu.VMEM((examples, queries), f32),
            pltpu.VMEM((rank, rank), f32),
            pltpu.VMEM((2, 32, 128), bf16),
            pltpu.VMEM((16, 32, 128), bf16),
            pltpu.VMEM((512, 128), f32),
            pltpu.VMEM((32, 128), f32),
            pltpu.VMEM((2, 16, 128), bf16),
            pltpu.VMEM((2, 16, 128), bf16),
            pltpu.VMEM((2, 4, 16, 128), bf16),
            pltpu.VMEM((4, 2, 4, 16, 128), bf16),
            pltpu.SemaphoreType.DMA((128,)),
            pltpu.SemaphoreType.DMA((128,)),
            pltpu.SemaphoreType.DMA,
            pltpu.SemaphoreType.DMA((10,)),
        ],
        compiler_params=pltpu.CompilerParams(
            collective_id=0, has_side_effects=True, vmem_limit_bytes=48 * 2**20
        ),
        cost_estimate=pl.CostEstimate(flops=4 * 10**9, bytes_accessed=14 * 10**6, transcendentals=0),
    )(hidden, grads, w_in, w_out, query)


def dot(a, b, precision=None):
    return lax.dot_general(
        a, b, (((1,), (0,)), ((), ())), preferred_element_type=f32, precision=precision
    )


def split(value):
    high = value.astype(bf16)
    return high, (value - high.astype(f32)).astype(bf16)


def solve_kernel(rows_of, rank, gram_ref, cross_ref, out_ref, product, inverse, sys_high, sys_low, answer):
    n = gram_ref.shape[0]
    gram = gram_ref[...]
    row = lax.broadcasted_iota(jnp.int32, (n, n), 0)
    col = lax.broadcasted_iota(jnp.int32, (n, n), 1)
    diagonal = row == col
    trace = jnp.sum(jnp.where(diagonal, gram, 0.0))
    damping = 0.1 * trace / n
    top = damping + jnp.minimum(trace, jnp.max(jnp.sum(jnp.abs(gram), axis=0)))
    system = gram + jnp.where(diagonal, damping, 0.0)
    scale = 2.0 / (damping + top)
    bound0 = (top - damping) / (top + damping)
    high, low = split(system)
    sys_high[...] = high
    sys_low[...] = low
    first, second = rows_of()
    shape = (8, n)
    want_row = lax.broadcasted_iota(jnp.int32, shape, 0)
    want_col = lax.broadcasted_iota(jnp.int32, shape, 1)
    unit = jnp.where(
        ((want_row == 0) & (want_col == first)) | ((want_row == 1) & (want_col == second)), 1.0, 0.0
    )

    def invert(multiply):
        def gain_of(bound):
            return 2.0 / (2.0 - bound * bound)

        def step(bound):
            gain = gain_of(bound)
            y = product[...]
            x = inverse[...]
            inverse[...] = gain * (2.0 * x - multiply(x, y))
            product[...] = gain * (2.0 * y - multiply(y, y))
            return bound * bound * 0.5 * gain

        gain = gain_of(bound0)
        y = scale * system
        inverse[...] = (gain * scale) * (jnp.where(diagonal, 2.0, 0.0) - y)
        product[...] = gain * (2.0 * y - multiply(y, y))
        lax.while_loop(lambda b: b > 0.06, step, bound0 * bound0 * 0.5 * gain)

    def apply(z, high, low):
        parts = jnp.concatenate(split(z), axis=0)
        whole = dot(parts, high) + dot(parts, low)
        return whole[:8] + whole[8:]

    def refine(correct, residual):
        def step(carry):
            z, left, _, count = carry
            z = z + correct(left)
            left = unit - residual(z)
            return z, left, jnp.max(jnp.abs(left)), count + 1

        def go_on(carry):
            return (carry[2] > 2e-5) & (carry[3] < 8)

        z, _, error, _ = lax.while_loop(
            go_on, step, (jnp.zeros(shape, f32), unit, jnp.float32(1.0), jnp.int32(0))
        )
        answer[...] = z
        return error

    def quick():
        invert(lambda a, b: dot(a.astype(bf16), b.astype(bf16)))
        near = inverse[...].astype(bf16)

        def correct(left):
            parts = jnp.concatenate(split(left), axis=0)
            moved = dot(parts, near)
            return moved[:8] + moved[8:]

        return refine(correct, lambda z: apply(z, sys_high[...], sys_low[...]))

    def careful():
        exact = lax.Precision.HIGHEST
        invert(lambda a, b: dot(a, b, exact))
        refine(
            lambda left: dot(left, inverse[...], exact),
            lambda z: dot(z, gram_ref[...], exact) + damping * z,
        )

    error = lax.cond(top < 500.0 * damping, quick, lambda: jnp.float32(1.0))
    pl.when(jnp.logical_not(error <= 2e-5))(careful)
    cross_high, cross_low = split(cross_ref[...])
    out_ref[...] = (damping / rank) * apply(answer[...], cross_high, cross_low)


def solve(gram, cross, rows_of, rank):
    n, nq = cross.shape
    return pl.pallas_call(
        functools.partial(solve_kernel, rows_of, rank),
        out_shape=jax.ShapeDtypeStruct((8, nq), f32),
        in_specs=[pl.BlockSpec(memory_space=pltpu.VMEM)] * 2,
        out_specs=pl.BlockSpec(memory_space=pltpu.VMEM),
        scratch_shapes=[
            pltpu.VMEM((n, n), f32),
            pltpu.VMEM((n, n), f32),
            pltpu.VMEM((n, n), bf16),
            pltpu.VMEM((n, n), bf16),
            pltpu.VMEM((8, n), f32),
        ],
        compiler_params=pltpu.CompilerParams(vmem_limit_bytes=40 * 2**20),
        cost_estimate=pl.CostEstimate(flops=2 * 10 * n**3, bytes_accessed=4 * n * (n + nq), transcendentals=0),
    )(gram, cross)


def shards(hidden, grads, w_in, w_out, query):
    gram, cross = gather(hidden, grads, w_in, w_out, query)

    def rows_of():
        x, y, z, c = place()
        first = (x * RINGS[1] + y) * 32 + z * 2 + c
        return first, first + 16

    return solve(gram, cross, rows_of, w_in.shape[0])[:2].T


def solution(mesh):
    in_specs = (
        P(("dp", "fsdp"), None),
        P(("dp", "fsdp"), None),
        P(None, "fsdp"),
        P(None, "fsdp"),
        P(("dp", "fsdp"), None),
    )
    out_specs = P(None, ("dp", "fsdp"))
    return jax.shard_map(shards, mesh=mesh, in_specs=in_specs, out_specs=out_specs, check_vma=False)
```

```python
import functools
import math
import jax
import jax.numpy as jnp
from jax import lax
from jax.experimental import pallas as pl
from jax.experimental.pallas import tpu as pltpu
from jax.sharding import PartitionSpec as P

LEN = 128
RINGS = (4, 4, 8)
LIMIT = 48 * 2**20
MESH = pl.DeviceIdType.MESH
f32, bf16 = jnp.float32, jnp.bfloat16


def dot_rows(a, b, precision=None):
    return lax.dot_general(
        a, b, (((1,), (1,)), ((), ())), preferred_element_type=f32, precision=precision
    )


def place():
    dp = lax.axis_index("dp")
    return lax.axis_index("fsdp"), lax.rem(lax.div(dp, 2), 4), lax.div(dp, 8), lax.rem(dp, 2)


def gather_kernel(
    hidden, grads, w_in, w_out, query,
    gram_out, cross_out,
    hid, grd, w_raw_in, w_raw_out, query_raw, weights, total,
    sketch_all, sketch_cols, query_all, query_cols, gram_pair, cross_pair,
    side, first_sent, first_got, spread, q_flat, q_sent, q_pair, q_x, q_y,
    send, got, first_sem, local,
):
    nx, ny, nz = RINGS
    x, y, z, c = place()
    other = 1 - c

    def at(dx=0, dy=0, dz=0, dc=0):
        px, py = lax.rem(x + (dx + nx), nx), lax.rem(y + (dy + ny), ny)
        pz, pc = lax.rem(z + (dz + nz), nz), lax.rem(c + dc, 2)
        return ((pz * ny + py) * 2 + pc, px)

    x_at = [x, lax.rem(x + 3, 4), lax.rem(x + 1, 4), lax.rem(x + 2, 4)]
    y_at = [y, lax.rem(y + 3, 4), lax.rem(y + 1, 4), lax.rem(y + 2, 4)]
    z_at = {k: lax.rem(z + k + nz, nz) for k in range(-4, 5)}

    partners = (
        [(k, 0, 0, 0) for k in (1, 2, 3)]
        + [(0, k, 0, 0) for k in (1, 2, 3)]
        + [(0, 0, k, j) for k in range(nz) for j in range(2) if k + j > 0]
    )
    barrier = pltpu.get_barrier_semaphore()
    for partner in partners:
        pl.semaphore_signal(barrier, inc=1, device_id=at(*partner), device_id_type=MESH)

    in_width, out_width = w_in.shape[1], w_out.shape[1]
    loads = []

    def load(src, dst):
        copy = pltpu.make_async_copy(src, dst, local.at[len(loads)])
        copy.start()
        loads.append(copy)
        return copy

    own_in = load(w_in, w_raw_in)
    own_out = load(w_out, w_raw_out)
    own_query = load(query, query_raw)
    sent = []
    count = [0]

    def message(src, dst, device, landing):
        number = count[0]
        count[0] += 1
        copy = pltpu.make_async_remote_copy(
            src_ref=src, dst_ref=dst, send_sem=send.at[number], recv_sem=got.at[number],
            device_id=device, device_id_type=MESH,
        )
        copy.start()
        sent.append(copy)
        return pltpu.make_async_remote_copy(
            src_ref=landing, dst_ref=landing, send_sem=send.at[number], recv_sem=got.at[number],
            device_id=device, device_id_type=MESH,
        )

    in_half, out_half = in_width // 2, out_width // 2
    own_in.wait()
    own_out.wait()
    hid_loads, grd_loads = [], []
    for k in range(4):
        hid_loads.append(load(hidden.at[:, pl.ds(pl.multiple_of(x_at[k] * in_width, 128), in_width)], hid.at[k]))
        grd_loads.append(load(grads.at[:, pl.ds(pl.multiple_of(x_at[k] * out_width, 128), out_width)], grd.at[k]))
    for raw, half, base in ((w_raw_in, in_half, 0), (w_raw_out, out_half, in_half)):
        for b in range(half // 128):
            pair = jnp.concatenate(
                [raw[:, 128 * b : 128 * (b + 1)], raw[:, half + 128 * b : half + 128 * (b + 1)]], axis=0
            )
            weights[0, base + 128 * b : base + 128 * (b + 1), :] = pair.T

    pl.semaphore_wait(barrier, len(partners))

    color = lax.rem(y, 2)
    per_core = (in_half + out_half) // 2
    starts, sizes = (0, 64, 192, 400), (64, 128, 208, 304)
    onward = {1: (0, 3), 2: (1, 2)}

    def piece(slot, core, which, part):
        begin = core * per_core + which * (per_core // 2) + starts[part]
        return weights.at[slot, pl.ds(pl.multiple_of(begin, 16), sizes[part]), :]

    def hop(slot, part):
        return message(
            piece(0, c, color, part), piece(slot, c, color, part), at(dx=1 if slot == 1 else -1),
            piece(slot, c, color, part),
        )

    order = [(slot, part) for part in range(4) for slot in (1, 2)]
    hops = {key: hop(*key) for key in order}

    own_query.wait()
    for b in range(32):
        q_flat[pl.ds(b, 1), :] = query_raw[:, 128 * b : 128 * (b + 1)].astype(f32)
    for h in range(2):
        q_sent[h] = q_flat[pl.ds(16 * h, 16), :].astype(bf16)
    q_a = message(q_sent.at[other], q_pair.at[c], at(dc=1), q_pair.at[other])
    q_pair[c] = q_sent[c]

    def product(k):
        values = (
            jnp.dot(hid[k, :, :in_half], weights[k, :in_half, :], preferred_element_type=f32),
            jnp.dot(hid[k, :, in_half:], weights[k, :in_half, :], preferred_element_type=f32),
            jnp.dot(grd[k, :, :out_half], weights[k, in_half:, :], preferred_element_type=f32),
            jnp.dot(grd[k, :, out_half:], weights[k, in_half:, :], preferred_element_type=f32),
        )
        for i, value in enumerate(values):
            total[i] = value if k == 0 else total[i] + value

    hid_loads[0].wait()
    grd_loads[0].wait()
    product(0)

    siblings = {1: [], 2: [], 3: []}
    crossing = {1: [], 2: [], 3: []}

    def to_sibling(slot, which, part):
        siblings[slot].append(
            message(piece(slot, c, which, part), piece(slot, c, which, part), at(dc=1), piece(slot, other, which, part))
        )

    def spread_out(slot, part):
        crossing[slot].append((part, message(
            piece(slot, c, color, part), piece(slot, c, color, part), at(dy=1 if part in onward[1] else -1),
            piece(slot, c, 1 - color, part),
        )))
        to_sibling(slot, color, part)

    far = []
    for slot, part in order:
        hops[slot, part].wait_recv()
        if part in onward[slot]:
            far.append((part, message(
                piece(slot, c, color, part), piece(3, c, color, part), at(dx=1 if slot == 1 else -1),
                piece(3, c, color, part),
            )))
        spread_out(slot, part)
        if (slot, part) == (2, 0):
            q_a.wait_recv()
            q_x[:, x] = q_pair[...]
            q_b = [
                message(q_pair, q_x.at[:, x], at(dx=k), q_x.at[:, lax.rem(x + nx - k, nx)]) for k in (1, 2, 3)
            ]

    def crossed(slot):
        for part, copy in crossing[slot]:
            copy.wait_recv()
            to_sibling(slot, 1 - color, part)

    for copy in q_b:
        copy.wait_recv()
    q_y[y] = q_x[...]
    q_c = [
        message(q_x, q_y.at[y], at(dy=k), q_y.at[lax.rem(y + ny - k, ny)]) for k in (1, 2, 3)
    ]
    for part, copy in far:
        copy.wait_recv()
        spread_out(3, part)
    crossed(1)
    crossed(2)
    def arrive(pair):
        for copy in pair:
            copy.wait_recv()

    q_rows = ny * 2 * nx

    def q_block(k):
        return query_all.at[pl.ds(pl.multiple_of(z_at[k] * q_rows, q_rows), q_rows), :]

    def q_half(k, h):
        return query_all.at[pl.ds(pl.multiple_of(z_at[k] * q_rows + h * (q_rows // 2), q_rows // 2), q_rows // 2), :]

    def q_step(t):
        if t < 4:
            return (
                message(q_block(1 - t), q_block(1 - t), at(dz=1), q_block(-t)),
                message(q_block(t - 1), q_block(t - 1), at(dz=-1), q_block(t)),
            )
        return (
            message(q_half(-3, 0), q_half(-3, 0), at(dz=1), q_half(-4, 0)),
            message(q_half(3, 1), q_half(3, 1), at(dz=-1), q_half(4, 1)),
        )

    def finish(slot):
        hid_loads[slot].wait()
        grd_loads[slot].wait()
        arrive(siblings[slot])
        product(slot)

    for copy in q_c:
        copy.wait_recv()
    spread[...] = q_y[...].reshape(ny * 2 * nx * 16, 128).astype(f32)
    for b in range(16):
        query_all[pl.ds(pl.multiple_of(z * q_rows, q_rows), q_rows), 128 * b : 128 * (b + 1)] = spread[
            pl.ds(b, q_rows, stride=16), :
        ].astype(bf16)

    q_ring = q_step(1)
    finish(1)
    crossed(3)
    finish(2)
    finish(3)
    arrive(q_ring)
    q_ring = q_step(2)

    rank = w_in.shape[0]
    in_side = total[0][:, :rank] + total[1][:, rank:]
    out_side = (total[2][:, :rank] + total[3][:, rank:]).T
    for s in range(2):
        tokens = slice(LEN * s, LEN * (s + 1))
        out_high, out_low = split(out_side[:, tokens])
        in_high, in_low = split(in_side[tokens, :])
        outer = jnp.dot(
            jnp.concatenate([out_high, out_high, out_low], axis=1),
            jnp.concatenate([in_high, in_low, in_high], axis=0), preferred_element_type=f32,
        )
        side[...] = outer / math.sqrt(LEN)
        rows = jnp.concatenate(
            [side[pl.ds(0, rank // 2, stride=2), :], side[pl.ds(1, rank // 2, stride=2), :]], axis=1
        ).astype(bf16)
        for h in range(2):
            first_sent[h, 16 * s : 16 * (s + 1), :] = rows[16 * h : 16 * (h + 1), :]

    slot = z * 2 + c
    first = []
    for dz in range(nz):
        for dc in range(2):
            if dz + dc > 0:
                copy = pltpu.make_async_remote_copy(
                    src_ref=first_sent.at[lax.rem(c + dc, 2)], dst_ref=first_got.at[slot],
                    send_sem=send.at[count[0]], recv_sem=first_sem, device_id=at(dz=dz, dc=dc), device_id_type=MESH,
                )
                count[0] += 1
                copy.start()
                sent.append(copy)
    first_got[slot] = first_sent[c]
    everyone = first_got.at[pl.ds(0, 2 * nz - 1)]
    pltpu.make_async_remote_copy(
        src_ref=everyone, dst_ref=everyone, send_sem=send.at[0], recv_sem=first_sem,
        device_id=at(dc=1), device_id_type=MESH,
    ).wait_recv()
    spread[...] = first_got[...].reshape(2 * nz * 32, 128).astype(f32)
    rows = 2 * 2 * nz

    def pick(on_first, on_second):
        return on_first + c * (on_second - on_first)

    u_at = [pick(a, b) for a, b in zip(y_at, x_at)]
    v_at = [pick(a, b) for a, b in zip(x_at, y_at)]

    def block(u, v):
        return sketch_all.at[pl.ds(pl.multiple_of((v_at[v] * nx + u_at[u]) * rows, rows), rows), :]

    def half(u, v, h):
        begin = (v_at[v] * nx + u_at[u]) * rows + h * (rows // 2)
        return sketch_all.at[pl.ds(pl.multiple_of(begin, rows // 2), rows // 2), :]

    def along_u(step):
        return at(dx=c * step, dy=other * step)

    def along_v(step):
        return at(dx=other * step, dy=c * step)

    for s in range(2):
        for b in range(16):
            begin = pl.multiple_of((v_at[0] * nx + u_at[0]) * rows + s * 16, 16)
            sketch_all[pl.ds(begin, 16), 128 * b : 128 * (b + 1)] = spread[
                pl.ds(s * 16 + b, 16, stride=32), :
            ].astype(bf16)

    u_left = message(block(0, 0), block(0, 0), along_u(1), block(1, 0))
    u_right = message(block(0, 0), block(0, 0), along_u(-1), block(2, 0))

    def send_v(u):
        return (
            message(block(u, 0), block(u, 0), along_v(1), block(u, 1)),
            message(block(u, 0), block(u, 0), along_v(-1), block(u, 2)),
        )

    def forward_v(u, pair):
        pair[0].wait_recv()
        left = message(half(u, 1, 0), half(u, 1, 0), along_v(1), half(u, 3, 0))
        pair[1].wait_recv()
        right = message(half(u, 2, 1), half(u, 2, 1), along_v(-1), half(u, 3, 1))
        return left, right

    slab = rows * nx
    gram_sums = []
    cross_sums = []

    def slab_at(v):
        return pl.ds(pl.multiple_of(v_at[v] * slab, slab), slab)

    def share(kind, pair, *index):
        kind.append(message(pair.at[(c,) + index], pair.at[(c,) + index], at(dc=1), pair.at[(other,) + index]))

    def multiply(v):
        here = slab_at(v)
        for b in range(16):
            lanes = slice(128 * b, 128 * (b + 1))
            sketch_cols[lanes, here] = sketch_all[here, lanes].T
        mine = sketch_all[here, :]
        if v < 3:
            for w in range(v + 1):
                there = slab_at(w)
                part = jnp.dot(mine, sketch_cols[:, there], preferred_element_type=f32)
                gram_pair[c, here, there] = part
                share(gram_sums, gram_pair, here, there)
                if w < v:
                    gram_pair[c, there, here] = part.T
                    share(gram_sums, gram_pair, there, here)
        else:
            gram_pair[c, here, :] = jnp.dot(mine, sketch_cols[...], preferred_element_type=f32)
            share(gram_sums, gram_pair, here, slice(None))
            for w in range(v):
                there = slab_at(w)
                gram_pair[c, there, here] = gram_pair[c, here, there].T
                share(gram_sums, gram_pair, there, here)

    def multiply_queries(v):
        here = slab_at(v)
        mine = sketch_all[here, :]
        cross_pair[c, here, :] = jnp.dot(mine, query_cols[...], preferred_element_type=f32)
        share(cross_sums, cross_pair, here, slice(None))

    u_far = message(block(0, 0), block(0, 0), along_u(2), block(3, 0))
    v_pairs = {0: send_v(0)}
    arrive(q_ring)
    q_ring = q_step(3)
    u_left.wait_recv()
    v_pairs[1] = send_v(1)
    u_right.wait_recv()
    v_pairs[2] = send_v(2)
    u_far.wait_recv()
    v_pairs[3] = send_v(3)
    multiply(0)
    tails = [forward_v(0, v_pairs[0])]
    arrive(q_ring)
    q_ring = q_step(4)
    for u in (1, 2, 3):
        tails.append(forward_v(u, v_pairs[u]))
    multiply(1)
    multiply(2)
    arrive(q_ring)
    for b in range(16):
        lanes = slice(128 * b, 128 * (b + 1))
        query_cols[lanes, :] = query_all[:, lanes].T
    for v in range(3):
        multiply_queries(v)
    for pair in tails:
        arrive(pair)
    multiply(3)
    multiply_queries(3)

    lane = lax.broadcasted_iota(jnp.int32, (rows, 128), 1)
    for copy in gram_sums:
        copy.wait_recv()
    for kx in range(nx):
        for ky in range(ny):
            source = slice((ky * nx + kx) * rows, (ky * nx + kx + 1) * rows)
            target = slice((kx * ny + ky) * rows, (kx * ny + ky + 1) * rows)
            tiles = [gram_pair[1, source, 128 * j : 128 * (j + 1)] for j in range(4)]
            for i in range(4):
                turned = tiles[i]
                for j in range(4):
                    if j != i:
                        moved = pltpu.roll(tiles[j], (32 * (j - i)) % 128, 1)
                        turned = jnp.where((lane >= 32 * j) & (lane < 32 * (j + 1)), moved, turned)
                lanes = slice(128 * i, 128 * (i + 1))
                gram_out[target, lanes] = gram_pair[0, target, lanes] + turned
    for copy in cross_sums:
        copy.wait_recv()
    for kx in range(nx):
        for ky in range(ny):
            source = slice((ky * nx + kx) * rows, (ky * nx + kx + 1) * rows)
            target = slice((kx * ny + ky) * rows, (kx * ny + ky + 1) * rows)
            cross_out[target, :] = cross_pair[0, target, :] + cross_pair[1, source, :]

    for copy in sent:
        copy.wait_send()


def gather(hidden, grads, w_in, w_out, query):
    examples, queries, half = 512, 256, 2048
    rank = w_in.shape[0]
    anywhere = pl.BlockSpec(memory_space=pltpu.HBM)
    vmem = pl.BlockSpec(memory_space=pltpu.VMEM)
    rows = hidden.shape[0]
    return pl.pallas_call(
        gather_kernel,
        out_shape=(
            jax.ShapeDtypeStruct((examples, examples), f32),
            jax.ShapeDtypeStruct((examples, queries), f32),
        ),
        in_specs=[anywhere] * 5,
        out_specs=(vmem, vmem),
        scratch_shapes=[
            pltpu.VMEM((4, rows, w_in.shape[1]), bf16),
            pltpu.VMEM((4, rows, w_out.shape[1]), bf16),
            pltpu.VMEM(w_in.shape, bf16),
            pltpu.VMEM(w_out.shape, bf16),
            pltpu.VMEM(query.shape, bf16),
            pltpu.VMEM((4, (w_in.shape[1] + w_out.shape[1]) // 2, 2 * rank), bf16),
            pltpu.VMEM((4, rows, 2 * rank), f32),
            pltpu.VMEM((examples, half), bf16),
            pltpu.VMEM((half, examples), bf16),
            pltpu.VMEM((queries, half), bf16),
            pltpu.VMEM((half, queries), bf16),
            pltpu.VMEM((2, examples, examples), f32),
            pltpu.VMEM((2, examples, queries), f32),
            pltpu.VMEM((rank, rank), f32),
            pltpu.VMEM((2, 32, 128), bf16),
            pltpu.VMEM((16, 32, 128), bf16),
            pltpu.VMEM((512, 128), f32),
            pltpu.VMEM((32, 128), f32),
            pltpu.VMEM((2, 16, 128), bf16),
            pltpu.VMEM((2, 16, 128), bf16),
            pltpu.VMEM((2, 4, 16, 128), bf16),
            pltpu.VMEM((4, 2, 4, 16, 128), bf16),
            pltpu.SemaphoreType.DMA((128,)),
            pltpu.SemaphoreType.DMA((128,)),
            pltpu.SemaphoreType.DMA,
            pltpu.SemaphoreType.DMA((11,)),
        ],
        compiler_params=pltpu.CompilerParams(
            collective_id=0, has_side_effects=True, vmem_limit_bytes=LIMIT
        ),
        cost_estimate=pl.CostEstimate(flops=4 * 10**9, bytes_accessed=14 * 10**6, transcendentals=0),
    )(hidden, grads, w_in, w_out, query)


def dot(a, b, precision=None):
    return lax.dot_general(
        a, b, (((1,), (0,)), ((), ())), preferred_element_type=f32, precision=precision
    )


def split(value):
    high = value.astype(bf16)
    return high, (value - high.astype(f32)).astype(bf16)


def solve_kernel(rows_of, rank, gram_ref, cross_ref, out_ref, product, inverse, sys_high, sys_low, answer):
    n = gram_ref.shape[0]
    gram = gram_ref[...]
    row = lax.broadcasted_iota(jnp.int32, (n, n), 0)
    col = lax.broadcasted_iota(jnp.int32, (n, n), 1)
    diagonal = row == col
    trace = jnp.sum(jnp.where(diagonal, gram, 0.0))
    damping = 0.1 * trace / n
    top = damping + jnp.minimum(trace, jnp.max(jnp.sum(jnp.abs(gram), axis=0)))
    system = gram + jnp.where(diagonal, damping, 0.0)
    scale = 2.0 / (damping + top)
    bound0 = (top - damping) / (top + damping)
    high, low = split(system)
    sys_high[...] = high
    sys_low[...] = low
    first, second = rows_of()
    shape = (8, n)
    want_row = lax.broadcasted_iota(jnp.int32, shape, 0)
    want_col = lax.broadcasted_iota(jnp.int32, shape, 1)
    unit = jnp.where(
        ((want_row == 0) & (want_col == first)) | ((want_row == 1) & (want_col == second)), 1.0, 0.0
    )

    def invert(multiply):
        def gain_of(bound):
            return 2.0 / (2.0 - bound * bound)

        def step(bound):
            gain = gain_of(bound)
            y = product[...]
            x = inverse[...]
            inverse[...] = gain * (2.0 * x - multiply(x, y))
            product[...] = gain * (2.0 * y - multiply(y, y))
            return bound * bound * 0.5 * gain

        gain = gain_of(bound0)
        y = scale * system
        inverse[...] = (gain * scale) * (jnp.where(diagonal, 2.0, 0.0) - y)
        product[...] = gain * (2.0 * y - multiply(y, y))
        lax.while_loop(lambda b: b > 0.06, step, bound0 * bound0 * 0.5 * gain)

    def apply(z, high, low):
        parts = jnp.concatenate(split(z), axis=0)
        whole = dot(parts, high) + dot(parts, low)
        return whole[:8] + whole[8:]

    def refine(correct, residual):
        def step(carry):
            z, left, _, count = carry
            z = z + correct(left)
            left = unit - residual(z)
            return z, left, jnp.max(jnp.abs(left)), count + 1

        def go_on(carry):
            return (carry[2] > 2e-5) & (carry[3] < 8)

        z, _, error, _ = lax.while_loop(
            go_on, step, (jnp.zeros(shape, f32), unit, jnp.float32(1.0), jnp.int32(0))
        )
        answer[...] = z
        return error

    def quick():
        invert(lambda a, b: dot(a.astype(bf16), b.astype(bf16)))
        near = inverse[...].astype(bf16)

        def correct(left):
            parts = jnp.concatenate(split(left), axis=0)
            moved = dot(parts, near)
            return moved[:8] + moved[8:]

        return refine(correct, lambda z: apply(z, sys_high[...], sys_low[...]))

    def careful():
        exact = lax.Precision.HIGHEST
        invert(lambda a, b: dot(a, b, exact))
        refine(
            lambda left: dot(left, inverse[...], exact),
            lambda z: dot(z, gram_ref[...], exact) + damping * z,
        )

    error = lax.cond(top < 500.0 * damping, quick, lambda: jnp.float32(1.0))
    pl.when(jnp.logical_not(error <= 2e-5))(careful)
    cross_high, cross_low = split(cross_ref[...])
    out_ref[...] = ((damping / rank) * apply(answer[...], cross_high, cross_low))[:2]


def solve(gram, cross, rows_of, rank):
    n, nq = cross.shape
    return pl.pallas_call(
        functools.partial(solve_kernel, rows_of, rank),
        out_shape=jax.ShapeDtypeStruct((2, nq), f32),
        in_specs=[pl.BlockSpec(memory_space=pltpu.VMEM)] * 2,
        out_specs=pl.BlockSpec(memory_space=pltpu.VMEM),
        scratch_shapes=[
            pltpu.VMEM((n, n), f32),
            pltpu.VMEM((n, n), f32),
            pltpu.VMEM((n, n), bf16),
            pltpu.VMEM((n, n), bf16),
            pltpu.VMEM((8, n), f32),
        ],
        compiler_params=pltpu.CompilerParams(vmem_limit_bytes=40 * 2**20),
        cost_estimate=pl.CostEstimate(flops=2 * 10 * n**3, bytes_accessed=4 * n * (n + nq), transcendentals=0),
    )(gram, cross)


def shards(hidden, grads, w_in, w_out, query):
    operands = (hidden, grads, w_in, w_out, query)
    gram, cross = gather(*(pltpu.with_memory_space_constraint(v, pltpu.HBM) for v in operands))

    def rows_of():
        x, y, z, c = place()
        first = (x * RINGS[1] + y) * 32 + z * 2 + c
        return first, first + 16

    return solve(gram, cross, rows_of, w_in.shape[0]).T


def solution(mesh):
    in_specs = (
        P(("dp", "fsdp"), None),
        P(("dp", "fsdp"), None),
        P(None, "fsdp"),
        P(None, "fsdp"),
        P(("dp", "fsdp"), None),
    )
    out_specs = P(None, ("dp", "fsdp"))
    return jax.shard_map(shards, mesh=mesh, in_specs=in_specs, out_specs=out_specs, check_vma=False)
```

```python
import functools
import math
import jax
import jax.numpy as jnp
from jax import lax
from jax.experimental import pallas as pl
from jax.experimental.pallas import tpu as pltpu
from jax.sharding import PartitionSpec as P

LEN = 128
RINGS = (4, 4, 8)
LIMIT = 48 * 2**20
MESH = pl.DeviceIdType.MESH
f32, bf16 = jnp.float32, jnp.bfloat16


def dot_rows(a, b, precision=None):
    return lax.dot_general(
        a, b, (((1,), (1,)), ((), ())), preferred_element_type=f32, precision=precision
    )


def place():
    dp = lax.axis_index("dp")
    return lax.axis_index("fsdp"), lax.rem(lax.div(dp, 2), 4), lax.div(dp, 8), lax.rem(dp, 2)


def gather_kernel(
    hidden, grads, w_in, w_out, query,
    gram_out, cross_out,
    hid, grd, w_raw_in, w_raw_out, query_raw, weights, total,
    sketch_all, sketch_cols, query_all, query_cols, gram_pair, cross_pair,
    side, first_sent, first_got, spread, q_flat, q_sent, q_pair, q_x, q_y,
    send, got, first_sem, local,
):
    nx, ny, nz = RINGS
    x, y, z, c = place()
    other = 1 - c

    def at(dx=0, dy=0, dz=0, dc=0):
        px, py = lax.rem(x + (dx + nx), nx), lax.rem(y + (dy + ny), ny)
        pz, pc = lax.rem(z + (dz + nz), nz), lax.rem(c + dc, 2)
        return ((pz * ny + py) * 2 + pc, px)

    x_at = [x, lax.rem(x + 3, 4), lax.rem(x + 1, 4), lax.rem(x + 2, 4)]
    y_at = [y, lax.rem(y + 3, 4), lax.rem(y + 1, 4), lax.rem(y + 2, 4)]
    z_at = {k: lax.rem(z + k + nz, nz) for k in range(-4, 5)}

    partners = (
        [(k, 0, 0, 0) for k in (1, 2, 3)]
        + [(0, k, 0, 0) for k in (1, 2, 3)]
        + [(0, 0, k, j) for k in range(nz) for j in range(2) if k + j > 0]
    )
    barrier = pltpu.get_barrier_semaphore()
    for partner in partners:
        pl.semaphore_signal(barrier, inc=1, device_id=at(*partner), device_id_type=MESH)

    in_width, out_width = w_in.shape[1], w_out.shape[1]
    loads = []

    def load(src, dst):
        copy = pltpu.make_async_copy(src, dst, local.at[len(loads)])
        copy.start()
        loads.append(copy)
        return copy

    own_in = load(w_in, w_raw_in)
    own_out = load(w_out, w_raw_out)
    own_query = load(query, query_raw)
    sent = []
    count = [0]

    def message(src, dst, device, landing):
        number = count[0]
        count[0] += 1
        copy = pltpu.make_async_remote_copy(
            src_ref=src, dst_ref=dst, send_sem=send.at[number], recv_sem=got.at[number],
            device_id=device, device_id_type=MESH,
        )
        copy.start()
        sent.append(copy)
        return pltpu.make_async_remote_copy(
            src_ref=landing, dst_ref=landing, send_sem=send.at[number], recv_sem=got.at[number],
            device_id=device, device_id_type=MESH,
        )

    in_half, out_half = in_width // 2, out_width // 2
    own_in.wait()
    own_out.wait()
    hid_loads, grd_loads = [], []
    for k in range(4):
        hid_loads.append(load(hidden.at[:, pl.ds(pl.multiple_of(x_at[k] * in_width, 128), in_width)], hid.at[k]))
        grd_loads.append(load(grads.at[:, pl.ds(pl.multiple_of(x_at[k] * out_width, 128), out_width)], grd.at[k]))
    for raw, half, base in ((w_raw_in, in_half, 0), (w_raw_out, out_half, in_half)):
        for b in range(half // 128):
            pair = jnp.concatenate(
                [raw[:, 128 * b : 128 * (b + 1)], raw[:, half + 128 * b : half + 128 * (b + 1)]], axis=0
            )
            weights[0, base + 128 * b : base + 128 * (b + 1), :] = pair.T

    pl.semaphore_wait(barrier, len(partners))

    color = lax.rem(y, 2)
    per_core = (in_half + out_half) // 2
    starts, sizes = (0, 176, 352, 528), (176, 176, 176, 176)
    onward = {1: (0, 3), 2: (1, 2)}

    def piece(slot, core, which, part):
        begin = core * per_core + which * (per_core // 2) + starts[part]
        return weights.at[slot, pl.ds(pl.multiple_of(begin, 16), sizes[part]), :]

    def hop(slot, part):
        return message(
            piece(0, c, color, part), piece(slot, c, color, part), at(dx=1 if slot == 1 else -1),
            piece(slot, c, color, part),
        )

    order = [(slot, part) for part in range(4) for slot in (1, 2)]
    hops = {key: hop(*key) for key in order}

    own_query.wait()
    for b in range(32):
        q_flat[pl.ds(b, 1), :] = query_raw[:, 128 * b : 128 * (b + 1)].astype(f32)
    for h in range(2):
        q_sent[h] = q_flat[pl.ds(16 * h, 16), :].astype(bf16)
    q_a = message(q_sent.at[other], q_pair.at[c], at(dc=1), q_pair.at[other])
    q_pair[c] = q_sent[c]

    def product(k):
        values = (
            jnp.dot(hid[k, :, :in_half], weights[k, :in_half, :], preferred_element_type=f32),
            jnp.dot(hid[k, :, in_half:], weights[k, :in_half, :], preferred_element_type=f32),
            jnp.dot(grd[k, :, :out_half], weights[k, in_half:, :], preferred_element_type=f32),
            jnp.dot(grd[k, :, out_half:], weights[k, in_half:, :], preferred_element_type=f32),
        )
        for i, value in enumerate(values):
            total[i] = value if k == 0 else total[i] + value

    hid_loads[0].wait()
    grd_loads[0].wait()
    product(0)

    siblings = {1: [], 2: [], 3: []}
    crossing = {1: [], 2: [], 3: []}

    def to_sibling(slot, which, part):
        siblings[slot].append(
            message(piece(slot, c, which, part), piece(slot, c, which, part), at(dc=1), piece(slot, other, which, part))
        )

    def spread_out(slot, part):
        crossing[slot].append((part, message(
            piece(slot, c, color, part), piece(slot, c, color, part), at(dy=1 if part in onward[1] else -1),
            piece(slot, c, 1 - color, part),
        )))
        to_sibling(slot, color, part)

    far = []
    for slot, part in order:
        hops[slot, part].wait_recv()
        if part in onward[slot]:
            far.append((part, message(
                piece(slot, c, color, part), piece(3, c, color, part), at(dx=1 if slot == 1 else -1),
                piece(3, c, color, part),
            )))
        spread_out(slot, part)
        if (slot, part) == (2, 0):
            q_a.wait_recv()
            q_x[:, x] = q_pair[...]
            q_b = [
                message(q_pair, q_x.at[:, x], at(dx=k), q_x.at[:, lax.rem(x + nx - k, nx)]) for k in (1, 2, 3)
            ]

    def crossed(slot):
        for part, copy in crossing[slot]:
            copy.wait_recv()
            to_sibling(slot, 1 - color, part)

    for copy in q_b:
        copy.wait_recv()
    q_y[y] = q_x[...]
    q_c = [
        message(q_x, q_y.at[y], at(dy=k), q_y.at[lax.rem(y + ny - k, ny)]) for k in (1, 2, 3)
    ]
    for part, copy in far:
        copy.wait_recv()
        spread_out(3, part)
    crossed(1)
    crossed(2)
    def arrive(pair):
        for copy in pair:
            copy.wait_recv()

    q_rows = ny * 2 * nx

    def q_block(k):
        return query_all.at[pl.ds(pl.multiple_of(z_at[k] * q_rows, q_rows), q_rows), :]

    def q_half(k, h):
        return query_all.at[pl.ds(pl.multiple_of(z_at[k] * q_rows + h * (q_rows // 2), q_rows // 2), q_rows // 2), :]

    def q_step(t):
        if t < 4:
            return (
                message(q_block(1 - t), q_block(1 - t), at(dz=1), q_block(-t)),
                message(q_block(t - 1), q_block(t - 1), at(dz=-1), q_block(t)),
            )
        return (
            message(q_half(-3, 0), q_half(-3, 0), at(dz=1), q_half(-4, 0)),
            message(q_half(3, 1), q_half(3, 1), at(dz=-1), q_half(4, 1)),
        )

    def finish(slot):
        hid_loads[slot].wait()
        grd_loads[slot].wait()
        arrive(siblings[slot])
        product(slot)

    for copy in q_c:
        copy.wait_recv()
    spread[...] = q_y[...].reshape(ny * 2 * nx * 16, 128).astype(f32)
    for b in range(16):
        query_all[pl.ds(pl.multiple_of(z * q_rows, q_rows), q_rows), 128 * b : 128 * (b + 1)] = spread[
            pl.ds(b, q_rows, stride=16), :
        ].astype(bf16)

    q_ring = q_step(1)
    finish(1)
    crossed(3)
    finish(2)
    finish(3)
    arrive(q_ring)
    q_ring = q_step(2)

    rank = w_in.shape[0]
    in_side = total[0][:, :rank] + total[1][:, rank:]
    out_side = (total[2][:, :rank] + total[3][:, rank:]).T
    for s in range(2):
        tokens = slice(LEN * s, LEN * (s + 1))
        out_high, out_low = split(out_side[:, tokens])
        in_high, in_low = split(in_side[tokens, :])
        outer = jnp.dot(
            jnp.concatenate([out_high, out_high, out_low], axis=1),
            jnp.concatenate([in_high, in_low, in_high], axis=0), preferred_element_type=f32,
        )
        side[...] = outer / math.sqrt(LEN)
        rows = jnp.concatenate(
            [side[pl.ds(0, rank // 2, stride=2), :], side[pl.ds(1, rank // 2, stride=2), :]], axis=1
        ).astype(bf16)
        for h in range(2):
            first_sent[h, 16 * s : 16 * (s + 1), :] = rows[16 * h : 16 * (h + 1), :]

    slot = z * 2 + c
    first = []
    for dz in range(nz):
        for dc in range(2):
            if dz + dc > 0:
                copy = pltpu.make_async_remote_copy(
                    src_ref=first_sent.at[lax.rem(c + dc, 2)], dst_ref=first_got.at[slot],
                    send_sem=send.at[count[0]], recv_sem=first_sem, device_id=at(dz=dz, dc=dc), device_id_type=MESH,
                )
                count[0] += 1
                copy.start()
                sent.append(copy)
    first_got[slot] = first_sent[c]
    everyone = first_got.at[pl.ds(0, 2 * nz - 1)]
    pltpu.make_async_remote_copy(
        src_ref=everyone, dst_ref=everyone, send_sem=send.at[0], recv_sem=first_sem,
        device_id=at(dc=1), device_id_type=MESH,
    ).wait_recv()
    spread[...] = first_got[...].reshape(2 * nz * 32, 128).astype(f32)
    rows = 2 * 2 * nz

    def pick(on_first, on_second):
        return on_first + c * (on_second - on_first)

    u_at = [pick(a, b) for a, b in zip(y_at, x_at)]
    v_at = [pick(a, b) for a, b in zip(x_at, y_at)]

    def block(u, v):
        return sketch_all.at[pl.ds(pl.multiple_of((v_at[v] * nx + u_at[u]) * rows, rows), rows), :]

    def half(u, v, h):
        begin = (v_at[v] * nx + u_at[u]) * rows + h * (rows // 2)
        return sketch_all.at[pl.ds(pl.multiple_of(begin, rows // 2), rows // 2), :]

    def along_u(step):
        return at(dx=c * step, dy=other * step)

    def along_v(step):
        return at(dx=other * step, dy=c * step)

    for s in range(2):
        for b in range(16):
            begin = pl.multiple_of((v_at[0] * nx + u_at[0]) * rows + s * 16, 16)
            sketch_all[pl.ds(begin, 16), 128 * b : 128 * (b + 1)] = spread[
                pl.ds(s * 16 + b, 16, stride=32), :
            ].astype(bf16)

    u_left = message(block(0, 0), block(0, 0), along_u(1), block(1, 0))
    u_right = message(block(0, 0), block(0, 0), along_u(-1), block(2, 0))

    def send_v(u):
        return (
            message(block(u, 0), block(u, 0), along_v(1), block(u, 1)),
            message(block(u, 0), block(u, 0), along_v(-1), block(u, 2)),
        )

    def forward_v(u, pair):
        pair[0].wait_recv()
        left = message(half(u, 1, 0), half(u, 1, 0), along_v(1), half(u, 3, 0))
        pair[1].wait_recv()
        right = message(half(u, 2, 1), half(u, 2, 1), along_v(-1), half(u, 3, 1))
        return left, right

    slab = rows * nx
    gram_sums = []
    cross_sums = []

    def slab_at(v):
        return pl.ds(pl.multiple_of(v_at[v] * slab, slab), slab)

    def share(kind, pair, *index):
        kind.append(message(pair.at[(c,) + index], pair.at[(c,) + index], at(dc=1), pair.at[(other,) + index]))

    def multiply(v):
        here = slab_at(v)
        for b in range(16):
            lanes = slice(128 * b, 128 * (b + 1))
            sketch_cols[lanes, here] = sketch_all[here, lanes].T
        mine = sketch_all[here, :]
        if v < 3:
            for w in range(v + 1):
                there = slab_at(w)
                part = jnp.dot(mine, sketch_cols[:, there], preferred_element_type=f32)
                gram_pair[c, here, there] = part
                share(gram_sums, gram_pair, here, there)
                if w < v:
                    gram_pair[c, there, here] = part.T
                    share(gram_sums, gram_pair, there, here)
        else:
            gram_pair[c, here, :] = jnp.dot(mine, sketch_cols[...], preferred_element_type=f32)
            share(gram_sums, gram_pair, here, slice(None))
            for w in range(v):
                there = slab_at(w)
                gram_pair[c, there, here] = gram_pair[c, here, there].T
                share(gram_sums, gram_pair, there, here)

    def multiply_queries(v):
        here = slab_at(v)
        mine = sketch_all[here, :]
        cross_pair[c, here, :] = jnp.dot(mine, query_cols[...], preferred_element_type=f32)
        share(cross_sums, cross_pair, here, slice(None))

    u_far = message(block(0, 0), block(0, 0), along_u(2), block(3, 0))
    v_pairs = {0: send_v(0)}
    arrive(q_ring)
    q_ring = q_step(3)
    u_left.wait_recv()
    v_pairs[1] = send_v(1)
    u_right.wait_recv()
    v_pairs[2] = send_v(2)
    u_far.wait_recv()
    v_pairs[3] = send_v(3)
    multiply(0)
    tails = [forward_v(0, v_pairs[0])]
    arrive(q_ring)
    q_ring = q_step(4)
    for u in (1, 2, 3):
        tails.append(forward_v(u, v_pairs[u]))
    multiply(1)
    multiply(2)
    arrive(q_ring)
    for b in range(16):
        lanes = slice(128 * b, 128 * (b + 1))
        query_cols[lanes, :] = query_all[:, lanes].T
    for v in range(3):
        multiply_queries(v)
    for pair in tails:
        arrive(pair)
    multiply(3)
    multiply_queries(3)

    lane = lax.broadcasted_iota(jnp.int32, (rows, 128), 1)
    for copy in gram_sums:
        copy.wait_recv()
    for kx in range(nx):
        for ky in range(ny):
            source = slice((ky * nx + kx) * rows, (ky * nx + kx + 1) * rows)
            target = slice((kx * ny + ky) * rows, (kx * ny + ky + 1) * rows)
            tiles = [gram_pair[1, source, 128 * j : 128 * (j + 1)] for j in range(4)]
            for i in range(4):
                turned = tiles[i]
                for j in range(4):
                    if j != i:
                        moved = pltpu.roll(tiles[j], (32 * (j - i)) % 128, 1)
                        turned = jnp.where((lane >= 32 * j) & (lane < 32 * (j + 1)), moved, turned)
                lanes = slice(128 * i, 128 * (i + 1))
                gram_out[target, lanes] = gram_pair[0, target, lanes] + turned
    for copy in cross_sums:
        copy.wait_recv()
    for kx in range(nx):
        for ky in range(ny):
            source = slice((ky * nx + kx) * rows, (ky * nx + kx + 1) * rows)
            target = slice((kx * ny + ky) * rows, (kx * ny + ky + 1) * rows)
            cross_out[target, :] = cross_pair[0, target, :] + cross_pair[1, source, :]

    for copy in sent:
        copy.wait_send()


def gather(hidden, grads, w_in, w_out, query):
    examples, queries, half = 512, 256, 2048
    rank = w_in.shape[0]
    anywhere = pl.BlockSpec(memory_space=pltpu.HBM)
    vmem = pl.BlockSpec(memory_space=pltpu.VMEM)
    rows = hidden.shape[0]
    return pl.pallas_call(
        gather_kernel,
        out_shape=(
            jax.ShapeDtypeStruct((examples, examples), f32),
            jax.ShapeDtypeStruct((examples, queries), f32),
        ),
        in_specs=[anywhere] * 5,
        out_specs=(vmem, vmem),
        scratch_shapes=[
            pltpu.VMEM((4, rows, w_in.shape[1]), bf16),
            pltpu.VMEM((4, rows, w_out.shape[1]), bf16),
            pltpu.VMEM(w_in.shape, bf16),
            pltpu.VMEM(w_out.shape, bf16),
            pltpu.VMEM(query.shape, bf16),
            pltpu.VMEM((4, (w_in.shape[1] + w_out.shape[1]) // 2, 2 * rank), bf16),
            pltpu.VMEM((4, rows, 2 * rank), f32),
            pltpu.VMEM((examples, half), bf16),
            pltpu.VMEM((half, examples), bf16),
            pltpu.VMEM((queries, half), bf16),
            pltpu.VMEM((half, queries), bf16),
            pltpu.VMEM((2, examples, examples), f32),
            pltpu.VMEM((2, examples, queries), f32),
            pltpu.VMEM((rank, rank), f32),
            pltpu.VMEM((2, 32, 128), bf16),
            pltpu.VMEM((16, 32, 128), bf16),
            pltpu.VMEM((512, 128), f32),
            pltpu.VMEM((32, 128), f32),
            pltpu.VMEM((2, 16, 128), bf16),
            pltpu.VMEM((2, 16, 128), bf16),
            pltpu.VMEM((2, 4, 16, 128), bf16),
            pltpu.VMEM((4, 2, 4, 16, 128), bf16),
            pltpu.SemaphoreType.DMA((128,)),
            pltpu.SemaphoreType.DMA((128,)),
            pltpu.SemaphoreType.DMA,
            pltpu.SemaphoreType.DMA((11,)),
        ],
        compiler_params=pltpu.CompilerParams(
            collective_id=0, has_side_effects=True, vmem_limit_bytes=LIMIT
        ),
        cost_estimate=pl.CostEstimate(flops=4 * 10**9, bytes_accessed=14 * 10**6, transcendentals=0),
    )(hidden, grads, w_in, w_out, query)


def dot(a, b, precision=None):
    return lax.dot_general(
        a, b, (((1,), (0,)), ((), ())), preferred_element_type=f32, precision=precision
    )


def split(value):
    high = value.astype(bf16)
    return high, (value - high.astype(f32)).astype(bf16)


def solve_kernel(rows_of, rank, gram_ref, cross_ref, out_ref, product, inverse, sys_high, sys_low, answer):
    n = gram_ref.shape[0]
    gram = gram_ref[...]
    row = lax.broadcasted_iota(jnp.int32, (n, n), 0)
    col = lax.broadcasted_iota(jnp.int32, (n, n), 1)
    diagonal = row == col
    trace = jnp.sum(jnp.where(diagonal, gram, 0.0))
    damping = 0.1 * trace / n
    top = damping + jnp.minimum(trace, jnp.max(jnp.sum(jnp.abs(gram), axis=0)))
    system = gram + jnp.where(diagonal, damping, 0.0)
    scale = 2.0 / (damping + top)
    bound0 = (top - damping) / (top + damping)
    high, low = split(system)
    sys_high[...] = high
    sys_low[...] = low
    first, second = rows_of()
    shape = (8, n)
    want_row = lax.broadcasted_iota(jnp.int32, shape, 0)
    want_col = lax.broadcasted_iota(jnp.int32, shape, 1)
    unit = jnp.where(
        ((want_row == 0) & (want_col == first)) | ((want_row == 1) & (want_col == second)), 1.0, 0.0
    )

    def invert(multiply):
        def gain_of(bound):
            return 2.0 / (2.0 - bound * bound)

        def step(bound):
            gain = gain_of(bound)
            y = product[...]
            x = inverse[...]
            inverse[...] = gain * (2.0 * x - multiply(x, y))
            product[...] = gain * (2.0 * y - multiply(y, y))
            return bound * bound * 0.5 * gain

        gain = gain_of(bound0)
        y = scale * system
        inverse[...] = (gain * scale) * (jnp.where(diagonal, 2.0, 0.0) - y)
        product[...] = gain * (2.0 * y - multiply(y, y))
        lax.while_loop(lambda b: b > 0.06, step, bound0 * bound0 * 0.5 * gain)

    def apply(z, high, low):
        parts = jnp.concatenate(split(z), axis=0)
        whole = dot(parts, high) + dot(parts, low)
        return whole[:8] + whole[8:]

    def refine(correct, residual):
        def step(carry):
            z, left, _, count = carry
            z = z + correct(left)
            left = unit - residual(z)
            return z, left, jnp.max(jnp.abs(left)), count + 1

        def go_on(carry):
            return (carry[2] > 2e-5) & (carry[3] < 8)

        z, _, error, _ = lax.while_loop(
            go_on, step, (jnp.zeros(shape, f32), unit, jnp.float32(1.0), jnp.int32(0))
        )
        answer[...] = z
        return error

    def quick():
        invert(lambda a, b: dot(a.astype(bf16), b.astype(bf16)))
        near = inverse[...].astype(bf16)

        def correct(left):
            parts = jnp.concatenate(split(left), axis=0)
            moved = dot(parts, near)
            return moved[:8] + moved[8:]

        return refine(correct, lambda z: apply(z, sys_high[...], sys_low[...]))

    def careful():
        exact = lax.Precision.HIGHEST
        invert(lambda a, b: dot(a, b, exact))
        refine(
            lambda left: dot(left, inverse[...], exact),
            lambda z: dot(z, gram_ref[...], exact) + damping * z,
        )

    error = lax.cond(top < 500.0 * damping, quick, lambda: jnp.float32(1.0))
    pl.when(jnp.logical_not(error <= 2e-5))(careful)
    cross_high, cross_low = split(cross_ref[...])
    out_ref[...] = ((damping / rank) * apply(answer[...], cross_high, cross_low))[:2]


def solve(gram, cross, rows_of, rank):
    n, nq = cross.shape
    return pl.pallas_call(
        functools.partial(solve_kernel, rows_of, rank),
        out_shape=jax.ShapeDtypeStruct((2, nq), f32),
        in_specs=[pl.BlockSpec(memory_space=pltpu.VMEM)] * 2,
        out_specs=pl.BlockSpec(memory_space=pltpu.VMEM),
        scratch_shapes=[
            pltpu.VMEM((n, n), f32),
            pltpu.VMEM((n, n), f32),
            pltpu.VMEM((n, n), bf16),
            pltpu.VMEM((n, n), bf16),
            pltpu.VMEM((8, n), f32),
        ],
        compiler_params=pltpu.CompilerParams(vmem_limit_bytes=40 * 2**20),
        cost_estimate=pl.CostEstimate(flops=2 * 10 * n**3, bytes_accessed=4 * n * (n + nq), transcendentals=0),
    )(gram, cross)


def shards(hidden, grads, w_in, w_out, query):
    operands = (hidden, grads, w_in, w_out, query)
    gram, cross = gather(*(pltpu.with_memory_space_constraint(v, pltpu.HBM) for v in operands))

    def rows_of():
        x, y, z, c = place()
        first = (x * RINGS[1] + y) * 32 + z * 2 + c
        return first, first + 16

    return solve(gram, cross, rows_of, w_in.shape[0]).T


def solution(mesh):
    in_specs = (
        P(("dp", "fsdp"), None),
        P(("dp", "fsdp"), None),
        P(None, "fsdp"),
        P(None, "fsdp"),
        P(("dp", "fsdp"), None),
    )
    out_specs = P(None, ("dp", "fsdp"))
    return jax.shard_map(shards, mesh=mesh, in_specs=in_specs, out_specs=out_specs, check_vma=False)
```
